1024 devices in a mesh: replica: 4 (over y_lo), fsdp: 256 (over y_hi, x, z, core).
Axes of the slice: x: 8, y: 8 (y_hi: 2, y_lo: 4; y = y_hi * 4 + y_lo), z: 8, core: 2. Of those that a mesh axis runs over, the one named last changes fastest.
Arguments:
- delta_codes: int32 [4, 8192, 128], P('replica', 'fsdp'), may hold values from 0 to 15
- scale_exponents: int32 [4, 8192, 4], P('replica', 'fsdp'), may hold values from -6 to -3
- error_feedback: float32 [4, 8192, 128], P('replica', 'fsdp'), may hold values from -0.3 to 0.3
- base_weights: float32 [8192, 128], P('fsdp'), may hold values from -5 to 5
- outer_momentum: float32 [8192, 128], P('fsdp'), may hold values from -1.2 to 1.2
- norm_gain: float32 [8192], replicated, may hold values from 0.1 to 1.9
- hidden_states: bfloat16 [4, 49152, 8192], P('replica', 'fsdp'), may hold values from -24 to 24
- key_cotangent: bfloat16 [4, 49152, 128], P('replica', 'fsdp'), may hold values from -8 to 8
Outputs:
- projected: bfloat16 [4, 49152, 128], P('replica', 'fsdp')
- weight_grad: float32 [4, 8192, 128], P('replica', 'fsdp')
- new_weights: float32 [8192, 128], P('fsdp')
- new_momentum: float32 [8192, 128], P('fsdp')
The draws below stay inside these ranges and needn't reach their ends.
All inputs are finite; a program needn't handle non-finite values.
Results may differ from the reference program's by a relative error of at most 0.0057.
Values may be sent and summed in bfloat16 or wider, within the bound.
A program may use at most 32 MiB of HBM per device.

```python
import math
import jax
import jax.numpy as jnp
from jax import lax

D = 8192
WIN = 128
BLOCK = 32
TOK_DEV = 192
REPLICAS = 4
TOKENS = 49152
N_FSDP = 256


def draw_hidden_states(key, part):
    key = jax.random.fold_in(key, 7)
    key_entries, key_columns, key_rows = jax.random.split(key, 3)
    extent = (REPLICAS, TOKENS, D)
    entries = jnp.clip(jax.random.normal(key_entries, extent, jnp.float32), -4.0, 4.0)
    spread = math.log(10.0)
    column_scale = jnp.exp(jax.random.uniform(key_columns, (D,), jnp.float32, -0.5 * spread, 0.5 * spread))
    row_scale = jnp.exp(jax.random.uniform(key_rows, (REPLICAS, TOKENS, 1), jnp.float32, -0.7, 0.7))
    return jnp.clip(entries * column_scale * row_scale, -24.0, 24.0).astype(jnp.bfloat16)


def touch_ends(values, own_key, low, high):
    longest = values.shape.index(max(values.shape))
    spots = []
    for shift in (0, 1):
        where = [jax.random.randint(jax.random.fold_in(own_key, axis), (), 0, length) for axis, length in enumerate(values.shape)]
        where[longest] = (where[longest] + shift) % values.shape[longest]
        spots.append(tuple(where))
    return values.at[spots[0]].set(low).at[spots[1]].set(high)


def block_levels(key, shape, cuts, least, top_value):
    gain, own = 1.0, jax.random.fold_in(key, 6)
    for position, parts in cuts:
        heights = jnp.exp(jax.random.uniform(jax.random.fold_in(own, position), (parts,), jnp.float32, least / len(cuts), top_value / len(cuts)))
        gain = gain * jnp.repeat(heights, shape[position] // parts).reshape([-1 if axis == position else 1 for axis in range(len(shape))])
    return gain


def scatter_about(stream_key, dims, width, limit, cuts=(), held_as=jnp.bfloat16):
    level = block_levels(stream_key, dims, cuts, -0.22, 0.18) if cuts else 1.0
    values = jax.random.normal(stream_key, dims, jnp.float32) * width * level
    return jnp.minimum(jnp.maximum(values, -limit), limit).astype(held_as)


def setup_inputs(seed: int = 0) -> dict:
    streams_of = jax.random.split(jax.random.key(seed), 9)
    delta_codes = touch_ends(jax.random.randint(streams_of[0], (REPLICAS, D, WIN), 0, 16), jax.random.fold_in(streams_of[0], 1), 0, 15).astype(jnp.int32)
    scale_exponents = touch_ends(jax.random.randint(streams_of[1], (REPLICAS, D, WIN // BLOCK), -6, -2), jax.random.fold_in(streams_of[1], 1), -6, (-2) - 1).astype(jnp.int32)
    error_feedback = scatter_about(streams_of[2], (REPLICAS, D, WIN), 0.05, 0.3, ((0, 4), (1, 256)), jnp.float32)
    base_weights = scatter_about(streams_of[3], (D, WIN), 1.0, 5.0, ((0, 256),), jnp.float32)
    outer_momentum = scatter_about(streams_of[4], (D, WIN), 0.2, 1.2, ((0, 256),), jnp.float32)
    norm_gain = jnp.clip(1.0 + 0.18 * jax.random.normal(streams_of[5], (D,), jnp.float32), 0.1, 1.9)
    hidden_states = draw_hidden_states(jax.random.fold_in(streams_of[8], 71), 0)
    key_cotangent = scatter_about(streams_of[7], (REPLICAS, TOKENS, WIN), 2.0, 8.0, ((0, 4), (1, 256)))
    return dict(delta_codes=delta_codes, scale_exponents=scale_exponents, error_feedback=error_feedback, base_weights=base_weights, outer_momentum=outer_momentum, norm_gain=norm_gain, hidden_states=hidden_states, key_cotangent=key_cotangent)


def decode(delta_codes, scale_exponents):
    polarity = jnp.where(delta_codes >= 8, 1.0, 0.0).astype(jnp.float32)
    polarity = 1.0 - 2.0 * polarity
    mantissa_code = delta_codes % 8
    exponent = mantissa_code // 2
    fraction = (mantissa_code % 2).astype(jnp.float32)
    magnitude = jnp.where(exponent == 0, 0.5 * fraction, jnp.exp2((exponent - 1).astype(jnp.float32)) * (1.0 + 0.5 * fraction))
    multiplier = jnp.exp2(scale_exponents.astype(jnp.float32))
    extent = delta_codes.shape
    blocked = (polarity * magnitude).reshape(extent[:-1] + (extent[-1] // BLOCK, BLOCK))
    return (blocked * multiplier[..., None]).reshape(extent)

def nesterov(outer_grad, base_weights, outer_momentum):
    new_momentum = 0.9 * outer_momentum + outer_grad
    new_weights = base_weights - 0.7 * (outer_grad + 0.9 * new_momentum)
    return (new_momentum, new_weights)

def rms_normed(hidden_block, norm_gain):
    widened = hidden_block.astype(jnp.float32)
    inverse = lax.rsqrt(lax.optimization_barrier(jnp.mean(widened * widened, axis=-1, keepdims=True)) + 1e-05)
    return (widened * inverse * norm_gain).astype(jnp.bfloat16)

def reference(delta_codes, scale_exponents, error_feedback, base_weights, outer_momentum, norm_gain, hidden_states, key_cotangent):
    summed = lax.optimization_barrier(jnp.sum(decode(delta_codes, scale_exponents) + error_feedback, axis=0))
    new_momentum, new_weights = nesterov(summed / REPLICAS, base_weights, outer_momentum)
    rounded_weights = new_weights.astype(jnp.bfloat16)
    multiplier = 1.0 / math.sqrt(D)
    grouping = math.gcd(N_FSDP, 16)
    block_size = TOK_DEV * grouping
    block_count = TOKENS // block_size

    def replica_pass(pieces):
        hidden_group, cotangent_group = pieces
        hidden_blocks = hidden_group.reshape(block_count, block_size, D)
        cotangent_blocks = cotangent_group.reshape(block_count, block_size, WIN)

        def advance(running, blocks):
            hidden_block, cotangent_block = blocks
            normed = rms_normed(hidden_block, norm_gain)
            projected = (jnp.dot(normed, rounded_weights, preferred_element_type=jnp.float32) * multiplier).astype(jnp.bfloat16)
            running = running + jnp.dot(normed.T, cotangent_block, preferred_element_type=jnp.float32)
            return (running, projected)
        running, projected = lax.scan(advance, jnp.zeros((D, WIN), jnp.float32), (hidden_blocks, cotangent_blocks))
        return (projected.reshape(TOKENS, WIN), running * multiplier)
    projected, weight_grad = lax.map(replica_pass, (hidden_states, key_cotangent))
    return (projected, weight_grad, new_weights, new_momentum)
```

```python
import functools
import math

import jax
import jax.numpy as jnp
from jax import lax
from jax.experimental import pallas as pl
from jax.experimental.pallas import tpu as pltpu
from jax.sharding import PartitionSpec as P

BLOCK = 32
ROWS = 32
PAIR = 2 * ROWS
LANES = 128
NQ = 2
NG = 2
NX = 4
MESH = pl.DeviceIdType.MESH
BF16 = jnp.bfloat16
F32 = jnp.float32


def decode(codes, exponents):
    lane = lax.broadcasted_iota(jnp.int32, codes.shape, 1)
    exponent = jnp.zeros(codes.shape, jnp.int32)
    for k in range(codes.shape[1] // BLOCK):
        exponent = jnp.where(lane // BLOCK == k, exponents[:, k : k + 1], exponent)
    scale = jnp.where(
        exponent == -6,
        2.0**-6,
        jnp.where(exponent == -5, 2.0**-5, jnp.where(exponent == -4, 2.0**-4, 2.0**-3)),
    ).astype(F32)
    magnitude_code = codes % 8
    level = magnitude_code // 2
    fraction = 0.5 * (magnitude_code % 2).astype(F32)
    magnitude = jnp.where(
        level == 0,
        fraction,
        jnp.where(level == 1, 1.0, jnp.where(level == 2, 2.0, 4.0)).astype(F32)
        * (1.0 + fraction),
    )
    return jnp.where(codes >= 8, -magnitude, magnitude) * scale


def kernel(
    replicas,
    n,
    tokens,
    codes_hbm,
    exps_hbm,
    err_hbm,
    base_hbm,
    mom_hbm,
    gain_hbm,
    hidden_hbm,
    cot_hbm,
    proj_ref,
    grad_ref,
    neww_ref,
    newm_ref,
    codes,
    exps,
    err,
    base,
    mom,
    gain,
    cot,
    hid,
    hother,
    cots,
    terms,
    wrows,
    wh,
    prod,
    total,
    rs_out,
    rs_in,
    rs2_out,
    rs2_in,
    rs3_out,
    rs3_in,
    part_out,
    part_in,
    load_sem,
    term_send,
    term_recv,
    hx_send,
    hx_recv,
    cx_sem,
    wy_send,
    wy_recv,
    ag1_send,
    ag1_recv,
    ag2_send,
    ag2_recv,
    rs_send,
    rs_recv,
    rs2_send,
    rs2_recv,
    rs3_send,
    rs3_recv,
    part_sem,
):
    half = n * n * PAIR
    h = n // 2
    model_width = 2 * half
    multiplier = 1.0 / math.sqrt(model_width)
    r = lax.axis_index("replica")
    index = lax.axis_index("fsdp")
    c = index % 2
    z = (index // 2) % n
    x = (index // (2 * n)) % n
    yh = index // (2 * n * n)
    me_a = (1 - c) * z + c * x
    me_b = (1 - c) * x + c * z

    def device(y_half, a, b):
        to_x = (1 - c) * b + c * a
        to_z = (1 - c) * a + c * b
        return (r, ((y_half * n + to_x) * n + to_z) * 2 + c)

    def on_chip(y_half, core):
        return (r, ((y_half * n + x) * n + z) * 2 + core)

    def along_a(step):
        return device(yh, lax.rem(me_a + step + n, n), me_b)

    def along_b(step):
        return device(yh, me_a, lax.rem(me_b + step + n, n))

    sibling = on_chip(yh, 1 - c)

    own = pl.ds(pl.multiple_of(c * half, half), half)
    others = pl.ds(pl.multiple_of((1 - c) * half, half), half)
    small = [
        (codes_hbm, codes),
        (exps_hbm, exps),
        (err_hbm, err),
        (base_hbm, base),
        (mom_hbm, mom),
        (gain_hbm, gain),
        (cot_hbm, cot),
    ]
    loads = [
        pltpu.make_async_copy(src, dst, load_sem.at[i])
        for i, (src, dst) in enumerate(small)
    ]
    load_own = pltpu.make_async_copy(
        hidden_hbm.at[:, own], hid.at[pl.ds(0, tokens)], load_sem.at[len(small)]
    )
    load_other = pltpu.make_async_copy(
        hidden_hbm.at[:, others], hother, load_sem.at[len(small) + 1]
    )

    barrier = pltpu.get_barrier_semaphore()
    partners = [(lax.rem(r + d, replicas), index) for d in range(1, replicas)]
    partners += [sibling, on_chip(1 - yh, 0), on_chip(1 - yh, 1)]
    partners += [along_a(d) for d in range(1, n)]
    partners += [along_b(d) for d in range(1, n)]
    for partner in partners:
        pl.semaphore_signal(barrier, inc=1, device_id=partner, device_id_type=MESH)
    for load in loads:
        load.start()
    load_own.start()
    load_other.start()

    for load in loads[:3]:
        load.wait()
    terms[r] = decode(codes[...], exps[...]) + err[...]
    for load in loads[3:]:
        load.wait()
    flat = index * ROWS
    gain_row = gain[pl.ds(flat // LANES, 1), :]
    lane = lax.broadcasted_iota(jnp.int32, (ROWS, LANES), 1)
    row = lax.broadcasted_iota(jnp.int32, (ROWS, LANES), 0)
    gain_col = jnp.sum(
        jnp.where(lane == row + lax.rem(flat, LANES), gain_row, 0.0),
        axis=1,
        keepdims=True,
    )

    pl.semaphore_wait(barrier, len(partners))

    def remote(src, dst, send, recv, to):
        return pltpu.make_async_remote_copy(
            src_ref=src,
            dst_ref=dst,
            send_sem=send,
            recv_sem=recv,
            device_id=to,
            device_id_type=MESH,
        )

    term_copies = []
    for d in range(1, replicas):
        copy = remote(
            terms.at[r],
            terms.at[r],
            term_send.at[d],
            term_recv.at[d],
            (lax.rem(r + d, replicas), index),
        )
        copy.start()
        term_copies.append(copy)
    hx_copies = []
    piece = tokens // NX
    for i in range(NX):
        copy = remote(
            hidden_hbm.at[pl.ds(i * piece, piece), others],
            hid.at[pl.ds(tokens + i * piece, piece)],
            hx_send.at[i],
            hx_recv.at[i],
            sibling,
        )
        copy.start()
        hx_copies.append(copy)

    load_own.wait()
    load_other.wait()
    inverse = []
    for g in range(tokens // 16):
        rows = pl.ds(g * 16, 16)
        square = jnp.zeros((16, LANES), F32)
        for ref in (hid, hother):
            for j in range(half // LANES):
                wide = ref[rows, j * LANES : (j + 1) * LANES].astype(F32)
                square = square + wide * wide
        mean = jnp.sum(square, axis=1, keepdims=True) * (1.0 / model_width)
        inv = lax.rsqrt(mean + 1e-05)
        inverse.append(inv)
        cots[rows, :] = (cot[rows, :].astype(F32) * inv).astype(BF16)
    cx_copy = remote(
        cots.at[pl.ds(0, tokens)],
        cots.at[pl.ds(tokens, tokens)],
        cx_sem.at[0],
        cx_sem.at[1],
        sibling,
    )
    cx_copy.start()

    for copy in term_copies:
        copy.wait_recv()
    summed = terms[0]
    for d in range(1, replicas):
        summed = summed + terms[d]
    outer_grad = summed / replicas
    new_momentum = 0.9 * mom[...] + outer_grad
    new_weights = base[...] - 0.7 * (outer_grad + 0.9 * new_momentum)
    newm_ref[...] = new_momentum
    neww_ref[...] = new_weights
    scaled_rows = (new_weights * gain_col).astype(BF16)
    wrows[...] = scaled_rows

    core_a = (1 - yh) * z + yh * x
    core_b = (1 - yh) * x + yh * z
    place = wh.at[core_b, core_a, pl.ds(pl.multiple_of(c * ROWS, ROWS), ROWS)]
    wy_far = remote(wrows, place, wy_send.at[0], wy_recv.at[c], on_chip(1 - yh, yh))
    wy_near = remote(wrows, place, wy_send.at[1], wy_recv.at[c], sibling)
    wy_far.start()

    @pl.when(c != yh)
    def _():
        wy_near.start()

    @pl.when(c == yh)
    def _():
        wh[core_b, core_a, pl.ds(pl.multiple_of(c * ROWS, ROWS), ROWS)] = scaled_rows

    def wy_wait(core):
        spot = wh.at[me_b, me_a, pl.ds(pl.multiple_of(core * ROWS, ROWS), ROWS)]
        remote(wrows, spot, wy_send.at[0], wy_recv.at[core], sibling).wait_recv()

    for copy in hx_copies:
        copy.wait_recv()
    cx_copy.wait_recv()
    cots_t = cots[...].T
    my_pair = me_a // 2

    def products(offset):
        p = lax.rem(my_pair + offset, h)
        for j in range(0, n, 2):
            tiles = []
            for t in (j, j + 1):
                at = (1 - c) * (t * n * PAIR + p * LANES) + c * (
                    p * 2 * n * PAIR + t * LANES
                )
                tiles.append(hid[:, pl.ds(pl.multiple_of(at, LANES), LANES)])
            out = jnp.dot(
                cots_t,
                jnp.concatenate(tiles, axis=1),
                preferred_element_type=F32,
            ).T
            for i, t in enumerate((j, j + 1)):
                for s in range(2):
                    a = 2 * p + (1 - c) * s + c * (t // h)
                    b = (1 - c) * t + c * (2 * (t % h) + s)
                    start = i * LANES + s * PAIR
                    prod[a, b] = out[start : start + PAIR]

    order = sorted(range(n), key=lambda d: -min(d, n - d))
    groups = [order[q * n // NQ : (q + 1) * n // NQ] for q in range(NQ)]
    rs_slots = {}
    for q in range(NQ):
        for k in range(h):
            for way in range(2):
                if k > 0 or way == 0:
                    rs_slots[q, way, k] = len(rs_slots)

    def rs_copy(q, way, k):
        slot = rs_slots[q, way, k]
        direction = 1 if (q + way) % 2 == 0 else -1
        return direction, remote(
            rs_out.at[slot],
            rs_in.at[slot],
            rs_send.at[slot],
            rs_recv.at[slot],
            along_a(direction),
        )

    def rs_step(k):
        for way in range(2):
            for q in range(NQ):
                if (q, way, k) not in rs_slots:
                    continue
                slot = rs_slots[q, way, k]
                direction, copy = rs_copy(q, way, k)
                to = lax.rem(me_a + direction * (h - k) + n, n)
                before = rs_slots.get((q, way, k - 1))
                if before is not None:
                    rs_copy(q, way, k - 1)[1].wait_recv()
                for i, d in enumerate(groups[q]):
                    value = prod[to, lax.rem(me_b + d, n)]
                    if before is not None:
                        value = value + rs_in[before, i].astype(F32)
                    rs_out[slot, i] = value.astype(BF16)
                copy.start()

    def rs2_copy(d):
        return remote(
            rs2_out.at[d], rs2_in.at[d], rs2_send.at[d], rs2_recv.at[d], along_b(d)
        )

    def rs_last(q):
        for way in range(2):
            if (q, way, h - 1) in rs_slots:
                rs_copy(q, way, h - 1)[1].wait_recv()
        for i, d in enumerate(groups[q]):
            value = prod[me_a, lax.rem(me_b + d, n)]
            for way in range(2):
                slot = rs_slots.get((q, way, h - 1))
                if slot is not None:
                    value = value + rs_in[slot, i].astype(F32)
            if d == 0:
                total[...] = value
            else:
                rs2_out[d] = value.astype(BF16)
                rs2_copy(d).start()

    def ag1_copy(d):
        spot = wh.at[me_b, me_a]
        return remote(spot, spot, ag1_send.at[d], ag1_recv.at[d], along_a(d))

    def ag1_wait(d):
        spot = wh.at[me_b, lax.rem(me_a - d + n, n)]
        remote(spot, spot, ag1_send.at[d], ag1_recv.at[d], along_a(d)).wait_recv()

    ag_slots = {}
    for q in range(NG):
        for k in range(h):
            for way in range(2):
                if k < h - 1 or way == 0:
                    ag_slots[q, way, k] = len(ag_slots)

    def ag_copy(q, way, k, received=False):
        slot = ag_slots[q, way, k]
        direction = 1 if (q + way) % 2 == 0 else -1
        back = k + 1 if received else k
        b = lax.rem(me_b - direction * back + n, n)
        spot = wh.at[b, pl.ds(q * n // NG, n // NG)]
        return remote(
            spot, spot, ag2_send.at[slot], ag2_recv.at[slot], along_b(direction)
        )

    def ag_step(k):
        for way in range(2):
            for q in range(NG):
                if (q, way, k - 1) in ag_slots:
                    ag_copy(q, way, k - 1, received=True).wait_recv()
                if (q, way, k) in ag_slots:
                    ag_copy(q, way, k).start()

    pairs = sorted(range(h), key=lambda d: -min(d, h - d))
    products(pairs[0])
    rs_step(0)
    wy_wait(1 - c)

    @pl.when(c != yh)
    def _():
        wy_wait(c)

    for d in order[:-1]:
        ag1_copy(d).start()
    for offset in pairs[1:]:
        products(offset)
    for k in range(1, h + 1):
        if k < h:
            rs_step(k)
        if k == 1:
            for d in order[:-1]:
                ag1_wait(d)
        ag_step(k - 1)
    for q in range(NQ):
        rs_last(q)
    ag_step(h)

    pieces = []
    for tx in range(n):
        for tz in range(n):
            pieces.append(wh[(1 - c) * tx + c * tz, (1 - c) * tz + c * tx])
    partial = jnp.dot(
        hid[...], jnp.concatenate(pieces, axis=0), preferred_element_type=F32
    )
    part_out[...] = partial[tokens:]
    part_copy = remote(part_out, part_in, part_sem.at[0], part_sem.at[1], sibling)
    part_copy.start()

    summed = total[...]
    for d in order[:-1]:
        rs2_copy(d).wait_recv()
        summed = summed + rs2_in[d].astype(F32)

    upper = summed[:ROWS]
    lower = summed[ROWS:]
    rs3_out[0] = upper
    rs3_out[1] = lower
    near = remote(
        rs3_out.at[1 - c], rs3_in.at[0], rs3_send.at[1 - c], rs3_recv.at[0], sibling
    )
    far = [
        remote(
            rs3_out.at[core],
            rs3_in.at[1],
            rs3_send.at[core],
            rs3_recv.at[1],
            on_chip(1 - yh, core),
        )
        for core in range(2)
    ]

    @pl.when(c == yh)
    def _():
        near.start()
        rs3_in[0] = rs3_out[c]

    @pl.when(c != yh)
    def _():
        far[0].start()
        far[1].start()

    part_copy.wait_recv()
    for g in range(tokens // 16):
        rows = slice(g * 16, g * 16 + 16)
        both = partial[rows] + part_in[rows, :]
        proj_ref[rows, :] = (both * (inverse[g] * multiplier)).astype(BF16)

    @pl.when(c != yh)
    def _():
        near.wait_recv()

    far[0].wait_recv()
    grad_ref[...] = (rs3_in[0] + rs3_in[1]) * (gain_col * multiplier)

    for copy in term_copies + hx_copies + [cx_copy, wy_far, part_copy]:
        copy.wait_send()

    @pl.when(c != yh)
    def _():
        wy_near.wait_send()
        far[0].wait_send()
        far[1].wait_send()

    @pl.when(c == yh)
    def _():
        near.wait_send()

    for d in range(1, n):
        ag1_copy(d).wait_send()
        rs2_copy(d).wait_send()
    for q, way, k in ag_slots:
        ag_copy(q, way, k).wait_send()
    for q, way, k in rs_slots:
        rs_copy(q, way, k)[1].wait_send()


def shards(
    replicas,
    n,
    delta_codes,
    scale_exponents,
    error_feedback,
    base_weights,
    outer_momentum,
    norm_gain,
    hidden_states,
    key_cotangent,
):
    tokens = hidden_states.shape[1]
    width = hidden_states.shape[2]
    half = width // 2
    h = n // 2
    any_space = pl.BlockSpec(memory_space=pl.ANY)
    vmem = pl.BlockSpec(memory_space=pltpu.VMEM)
    dma = pltpu.SemaphoreType.DMA
    rs_count = NQ * (2 * h - 1)
    ag_count = NG * (2 * h - 1)
    outs = pl.pallas_call(
        functools.partial(kernel, replicas, n, tokens),
        out_shape=(
            jax.ShapeDtypeStruct((tokens, LANES), BF16),
            jax.ShapeDtypeStruct((ROWS, LANES), F32),
            jax.ShapeDtypeStruct((ROWS, LANES), F32),
            jax.ShapeDtypeStruct((ROWS, LANES), F32),
        ),
        in_specs=[any_space] * 8,
        out_specs=(vmem,) * 4,
        scratch_shapes=[
            pltpu.VMEM((ROWS, LANES), jnp.int32),
            pltpu.VMEM((ROWS, LANES // BLOCK), jnp.int32),
            pltpu.VMEM((ROWS, LANES), F32),
            pltpu.VMEM((ROWS, LANES), F32),
            pltpu.VMEM((ROWS, LANES), F32),
            pltpu.VMEM((width // LANES, LANES), F32),
            pltpu.VMEM((tokens, LANES), BF16),
            pltpu.VMEM((2 * tokens, half), BF16),
            pltpu.VMEM((tokens, half), BF16),
            pltpu.VMEM((2 * tokens, LANES), BF16),
            pltpu.VMEM((replicas, ROWS, LANES), F32),
            pltpu.VMEM((ROWS, LANES), BF16),
            pltpu.VMEM((n, n, PAIR, LANES), BF16),
            pltpu.VMEM((n, n, PAIR, LANES), F32),
            pltpu.VMEM((PAIR, LANES), F32),
            pltpu.VMEM((rs_count, n // NQ, PAIR, LANES), BF16),
            pltpu.VMEM((rs_count, n // NQ, PAIR, LANES), BF16),
            pltpu.VMEM((n, PAIR, LANES), BF16),
            pltpu.VMEM((n, PAIR, LANES), BF16),
            pltpu.VMEM((2, ROWS, LANES), F32),
            pltpu.VMEM((2, ROWS, LANES), F32),
            pltpu.VMEM((tokens, LANES), F32),
            pltpu.VMEM((tokens, LANES), F32),
            dma((9,)),
            dma((replicas,)),
            dma((replicas,)),
            dma((NX,)),
            dma((NX,)),
            dma((2,)),
            dma((2,)),
            dma((2,)),
            dma((n,)),
            dma((n,)),
            dma((ag_count,)),
            dma((ag_count,)),
            dma((rs_count,)),
            dma((rs_count,)),
            dma((n,)),
            dma((n,)),
            dma((2,)),
            dma((2,)),
            dma((2,)),
        ],
        compiler_params=pltpu.CompilerParams(
            collective_id=0, has_side_effects=True, vmem_limit_bytes=40 * 1024 * 1024
        ),
        cost_estimate=pl.CostEstimate(
            flops=4 * tokens * width * LANES,
            bytes_accessed=2 * tokens * width,
            transcendentals=tokens,
        ),
    )(
        delta_codes[0],
        scale_exponents[0],
        error_feedback[0],
        base_weights,
        outer_momentum,
        norm_gain.reshape(width // LANES, LANES),
        hidden_states[0],
        key_cotangent[0],
    )
    projected, weight_grad, new_weights, new_momentum = outs
    return (projected[None], weight_grad[None], new_weights, new_momentum)


def solution(mesh):
    replicas = mesh.shape["replica"]
    n = math.isqrt(mesh.shape["fsdp"] // 4)
    return jax.shard_map(
        functools.partial(shards, replicas, n),
        mesh=mesh,
        in_specs=(
            P("replica", "fsdp", None),
            P("replica", "fsdp", None),
            P("replica", "fsdp", None),
            P("fsdp", None),
            P("fsdp", None),
            P(),
            P("replica", "fsdp", None),
            P("replica", "fsdp", None),
        ),
        out_specs=(
            P("replica", "fsdp", None),
            P("replica", "fsdp", None),
            P("fsdp", None),
            P("fsdp", None),
        ),
        check_vma=False,
    )
```

```python
import functools
import math

import jax
import jax.numpy as jnp
from jax import lax
from jax.experimental import pallas as pl
from jax.experimental.pallas import tpu as pltpu
from jax.sharding import PartitionSpec as P

BLOCK = 32
ROWS = 32
PAIR = 2 * ROWS
LANES = 128
NX = 4
VMEM_BYTES = 63 * 1024 * 1024
MESH = pl.DeviceIdType.MESH
BF16 = jnp.bfloat16
F32 = jnp.float32


def column(line, start):
    shape = (ROWS, line.shape[1])
    lane = lax.broadcasted_iota(jnp.int32, shape, 1)
    row = lax.broadcasted_iota(jnp.int32, shape, 0)
    return jnp.sum(jnp.where(lane == row + start, line, 0.0), axis=1, keepdims=True)


def decode(codes, exponents):
    powers = jnp.where(
        exponents == -6,
        2.0**-6,
        jnp.where(
            exponents == -5, 2.0**-5, jnp.where(exponents == -4, 2.0**-4, 2.0**-3)
        ),
    ).astype(F32)
    lane = lax.broadcasted_iota(jnp.int32, codes.shape, 1)
    scale = jnp.zeros(codes.shape, F32)
    for k in range(codes.shape[1] // BLOCK):
        scale = jnp.where(lane // BLOCK == k, column(powers[k : k + 1], 0), scale)
    magnitude_code = codes % 8
    level = magnitude_code // 2
    fraction = 0.5 * (magnitude_code % 2).astype(F32)
    magnitude = jnp.where(
        level == 0,
        fraction,
        jnp.where(level == 1, 1.0, jnp.where(level == 2, 2.0, 4.0)).astype(F32)
        * (1.0 + fraction),
    )
    return jnp.where(codes >= 8, -magnitude, magnitude) * scale


def ring_plan(n):
    if n == 8:
        return [1], 2, [3]
    if n == 4:
        return [], 1, []
    raise ValueError(n)


def kernel(
    replicas,
    n,
    tokens,
    codes_hbm,
    exps_hbm,
    err_hbm,
    base_hbm,
    mom_hbm,
    gain_hbm,
    hidden_hbm,
    cot_hbm,
    proj_ref,
    grad_ref,
    neww_ref,
    newm_ref,
    codes,
    exps,
    err,
    base,
    mom,
    gain,
    cot,
    hid,
    hother,
    cots,
    terms,
    share,
    shares,
    wh,
    prod,
    rs_out,
    rs_in,
    last_out,
    last_in,
    part_out,
    part_in,
    load_sem,
    term_send,
    term_recv,
    hx_send,
    hx_recv,
    cx_sem,
    share_send,
    share_recv,
    ag1_send,
    ag1_recv,
    ag2_send,
    ag2_recv,
    rs_send,
    rs_recv,
    last_send,
    last_recv,
    part_sem,
    ready_sem,
):
    half = n * n * PAIR
    h = n // 2
    direct, middle, further = ring_plan(n)
    model_width = 2 * half
    multiplier = 1.0 / math.sqrt(model_width)
    r = lax.axis_index("replica")
    index = lax.axis_index("fsdp")
    c = index % 2
    z = (index // 2) % n
    x = (index // (2 * n)) % n
    yh = index // (2 * n * n)
    me_a = (1 - c) * z + c * x
    me_b = (1 - c) * x + c * z

    def device(y_half, a, b, core):
        to_x = (1 - c) * b + c * a
        to_z = (1 - c) * a + c * b
        return (r, ((y_half * n + to_x) * n + to_z) * 2 + core)

    def on_column(step, y_half, core):
        return (lax.rem(r + step, replicas), ((y_half * n + x) * n + z) * 2 + core)

    def along_a(step):
        return device(yh, lax.rem(me_a + step + n, n), me_b, c)

    def along_b(step):
        return device(yh, me_a, lax.rem(me_b + step + n, n), c)

    sibling = on_column(0, yh, 1 - c)

    own = pl.ds(pl.multiple_of(c * half, half), half)
    others = pl.ds(pl.multiple_of((1 - c) * half, half), half)
    small = [
        (codes_hbm, codes),
        (exps_hbm, exps),
        (err_hbm, err),
        (base_hbm, base),
        (mom_hbm, mom),
        (gain_hbm, gain),
        (cot_hbm, cot),
    ]
    loads = [
        pltpu.make_async_copy(src, dst, load_sem.at[i])
        for i, (src, dst) in enumerate(small)
    ]
    load_own = pltpu.make_async_copy(
        hidden_hbm.at[:, own], hid.at[pl.ds(0, tokens)], load_sem.at[len(small)]
    )
    load_other = pltpu.make_async_copy(
        hidden_hbm.at[:, others], hother, load_sem.at[len(small) + 1]
    )

    barrier = pltpu.get_barrier_semaphore()
    partners = [on_column(0, 1 - yh, 0), on_column(0, 1 - yh, 1), sibling]
    for d in range(1, replicas):
        for y_half in range(2):
            for core in range(2):
                partners.append(on_column(d, y_half, core))
    partners += [along_a(d) for d in range(1, n)]
    partners += [along_b(d) for d in range(1, n)]
    for partner in partners:
        pl.semaphore_signal(barrier, inc=1, device_id=partner, device_id_type=MESH)
    for load in loads:
        load.start()
    load_own.start()
    load_other.start()

    for load in loads:
        load.wait()
    term = decode(codes[...], exps[...]) + err[...]
    terms[r] = term
    flat = index * ROWS
    gain_col = column(gain[pl.ds(flat // LANES, 1), :], lax.rem(flat, LANES))
    kept = (base[...] - (0.7 * 0.9 * 0.9) * mom[...]) * (1.0 / replicas)
    my_share = ((kept - (0.7 * 1.9 / replicas) * term) * gain_col).astype(BF16)
    share[...] = my_share

    pl.semaphore_wait(barrier, len(partners))

    def remote(src, dst, send, recv, to):
        return pltpu.make_async_remote_copy(
            src_ref=src,
            dst_ref=dst,
            send_sem=send,
            recv_sem=recv,
            device_id=to,
            device_id_type=MESH,
        )

    def share_copy(d, flip):
        y_half = (1 - yh) * flip + yh * (1 - flip)
        return remote(
            share,
            shares.at[r, c],
            share_send.at[d, flip],
            share_recv.at[r, c],
            on_column(d, y_half, yh),
        )

    share_spots = [(d, flip) for d in range(replicas) for flip in range(2)]
    for d, flip in share_spots[1:]:
        share_copy(d, flip).start()

    @pl.when(c != yh)
    def _():
        share_copy(0, 0).start()

    @pl.when(c == yh)
    def _():
        shares[r, c] = my_share

    hx_copies = []
    piece = tokens // NX
    for i in range(NX):
        copy = remote(
            hidden_hbm.at[pl.ds(i * piece, piece), others],
            hid.at[pl.ds(tokens + i * piece, piece)],
            hx_send.at[i],
            hx_recv.at[i],
            sibling,
        )
        copy.start()
        hx_copies.append(copy)
    term_copies = []
    for d in range(1, replicas):
        copy = remote(
            terms.at[r],
            terms.at[r],
            term_send.at[d],
            term_recv.at[d],
            on_column(d, yh, c),
        )
        copy.start()
        term_copies.append(copy)
    for d in range(1, n):
        pl.semaphore_signal(
            ready_sem, inc=1, device_id=along_b(d), device_id_type=MESH
        )

    load_own.wait()
    load_other.wait()
    inverse = []
    for g in range(tokens // 16):
        rows = pl.ds(g * 16, 16)
        square = jnp.zeros((16, LANES), F32)
        for ref in (hid, hother):
            for j in range(half // LANES):
                wide = ref[rows, j * LANES : (j + 1) * LANES].astype(F32)
                square = square + wide * wide
        mean = jnp.sum(square, axis=1, keepdims=True) * (1.0 / model_width)
        inv = lax.rsqrt(mean + 1e-05)
        inverse.append(inv)
        cots[rows, :] = (cot[rows, :].astype(F32) * inv).astype(BF16)
    cx_copy = remote(
        cots.at[pl.ds(0, tokens)],
        cots.at[pl.ds(tokens, tokens)],
        cx_sem.at[0],
        cx_sem.at[1],
        sibling,
    )
    cx_copy.start()

    for copy in hx_copies:
        copy.wait_recv()
    cx_copy.wait_recv()
    cots_t = cots[...].T
    my_pair = me_a // 2

    def products(offset):
        p = lax.rem(my_pair + offset, h)
        for j in range(0, n, 2):
            tiles = []
            for t in (j, j + 1):
                at = (1 - c) * (t * n * PAIR + p * LANES) + c * (
                    p * 2 * n * PAIR + t * LANES
                )
                tiles.append(hid[:, pl.ds(pl.multiple_of(at, LANES), LANES)])
            out = jnp.dot(
                cots_t,
                jnp.concatenate(tiles, axis=1),
                preferred_element_type=F32,
            ).T
            for i, t in enumerate((j, j + 1)):
                for s in range(2):
                    a = 2 * p + (1 - c) * s + c * (t // h)
                    b = (1 - c) * t + c * (2 * (t % h) + s)
                    start = i * LANES + s * PAIR
                    prod[a, b] = out[start : start + PAIR]

    order = sorted(range(n), key=lambda d: -min(d, n - d))
    groups = [order[:h], order[h:]]
    ways = (1, -1)
    rs_slots = {}
    for q in range(2):
        if middle < h:
            rs_slots["far", q, ways[q], h] = len(rs_slots)
        for s in ways:
            for d in further:
                rs_slots["far", q, s, d] = len(rs_slots)
    for q in range(2):
        for s in ways:
            for d in [middle] + direct:
                rs_slots["near", q, s, d] = len(rs_slots)

    def rs_copy(key):
        kind, _, s, d = key
        slot = rs_slots[key]
        return remote(
            rs_out.at[slot],
            rs_in.at[slot],
            rs_send.at[slot],
            rs_recv.at[slot],
            along_a(s * (d - middle) if kind == "far" else s * d),
        )

    def rs_send_block(key):
        kind, q, s, d = key
        to = lax.rem(me_a + s * d + n, n)
        arrived = []
        if kind == "near" and d == middle:
            arrived = [k for k in rs_slots if k[0] == "far" and k[1:3] == (q, s)]
            for k in arrived:
                rs_copy(k).wait_recv()
        for i, e in enumerate(groups[q]):
            value = prod[to, lax.rem(me_b + e, n)]
            for k in arrived:
                value = value + rs_in[rs_slots[k], i].astype(F32)
            rs_out[rs_slots[key], i] = value.astype(BF16)
        rs_copy(key).start()

    def rs_sends(kind, distances):
        for key in rs_slots:
            if key[0] == kind and key[3] in distances:
                rs_send_block(key)

    def last_copy(e, core):
        return remote(
            last_out.at[e, core],
            last_in.at[yh, e],
            last_send.at[e, core],
            last_recv.at[yh, e],
            device(c, me_a, lax.rem(me_b + e, n), core),
        )

    def rs_last(q):
        keys = [k for k in rs_slots if k[0] == "near" and k[1] == q]
        for k in keys:
            rs_copy(k).wait_recv()
        for i, e in enumerate(groups[q]):
            value = prod[me_a, lax.rem(me_b + e, n)]
            for k in keys:
                value = value + rs_in[rs_slots[k], i].astype(F32)
            value = value.astype(BF16)
            last_out[e, 0] = value[:ROWS]
            last_out[e, 1] = value[ROWS:]
            if e > 0:
                last_copy(e, 0).start()
                last_copy(e, 1).start()
            else:

                @pl.when(c != yh)
                def _():
                    last_copy(0, 0).start()
                    last_copy(0, 1).start()

                @pl.when(c == yh)
                def _():
                    last_copy(0, 1 - c).start()
                    last_in[yh, 0] = last_out[0, c]

    def last_wait(y_half, e):
        spot = last_in.at[y_half, e]
        remote(
            last_out.at[0, 0],
            spot,
            last_send.at[0, 0],
            last_recv.at[y_half, e],
            sibling,
        ).wait_recv()

    nearest = order[::-1]
    place = {d: i for i, d in enumerate(nearest)}

    def ag1_copy(d):
        return remote(
            wh.at[0, 0],
            wh.at[0, place[n - d]],
            ag1_send.at[d],
            ag1_recv.at[d],
            along_a(d),
        )

    ag_slots = {}
    for g in range(2):
        for s in ways:
            for d in [middle] + direct:
                ag_slots["near", g, s, d] = len(ag_slots)
        for s in ways:
            for d in further + [h]:
                ag_slots["far", g, s, d] = len(ag_slots)

    def ag_copy(key):
        kind, g, s, d = key
        first, count = g * h, h
        if d == h:
            count = h // 2
            first += count * (s < 0)
        blocks = pl.ds(first, count)
        came, hops = (0, d) if kind == "near" else (middle, d - middle)
        slot = ag_slots[key]
        return remote(
            wh.at[(-s * came) % n, blocks],
            wh.at[(-s * d) % n, blocks],
            ag2_send.at[slot],
            ag2_recv.at[slot],
            along_b(s * hops),
        )

    def ag_near(g):
        for d in nearest[g * h : (g + 1) * h]:
            if d > 0:
                ag1_copy(n - d).wait_recv()
        for key in ag_slots:
            if key[:2] == ("near", g):
                ag_copy(key).start()

    def ag_far(g):
        for s in ways:
            ag_copy(("near", g, s, middle)).wait_recv()
            for d in further + [h]:
                ag_copy(("far", g, s, d)).start()

    pairs = sorted(range(h), key=lambda d: -min(d, h - d))
    for offset in pairs[:-1]:
        products(offset)
    rs_sends("far", [h])
    rs_sends("far", further)
    products(pairs[-1])

    @pl.when(c != yh)
    def _():
        remote(
            share, shares.at[r, c], share_send.at[0, 0], share_recv.at[r, c], sibling
        ).wait_recv()

    for d in range(replicas):
        for other in range(2):
            if (d, other) != (0, 0):
                source = lax.rem(r + d, replicas)
                core = (c + other) % 2
                remote(
                    share,
                    shares.at[source, core],
                    share_send.at[0, 0],
                    share_recv.at[source, core],
                    sibling,
                ).wait_recv()
    for core in range(2):
        rows64 = shares[0, core].astype(F32)
        for d in range(1, replicas):
            rows64 = rows64 + shares[d, core].astype(F32)
        wh[0, 0, pl.ds(core * ROWS, ROWS)] = rows64.astype(BF16)
    for d in nearest[1:]:
        ag1_copy(d).start()

    rs_sends("near", direct)
    ag_near(0)
    rs_sends("near", [middle])
    ag_near(1)
    ag_far(0)

    for copy in term_copies:
        copy.wait_recv()
    summed = terms[0]
    for d in range(1, replicas):
        summed = summed + terms[d]
    outer_grad = summed / replicas
    new_momentum = 0.9 * mom[...] + outer_grad
    newm_ref[...] = new_momentum
    neww_ref[...] = base[...] - 0.7 * (outer_grad + 0.9 * new_momentum)

    pl.semaphore_wait(ready_sem, n - 1)
    rs_last(0)
    rs_last(1)
    ag_far(1)
    for key in ag_slots:
        if key[0] == "far" or key[3] != middle:
            ag_copy(key).wait_recv()

    pieces = []
    for tx in range(n):
        for tz in range(n):
            a = (1 - c) * tz + c * tx
            b = (1 - c) * tx + c * tz
            rel_a = lax.rem(a - me_a + n, n)
            rel_b = lax.rem(b - me_b + n, n)
            pieces.append((rel_b, rel_a))
    tiles = []
    for rel_b, rel_a in pieces:
        back = rel_a // h
        at = (1 - back) * 2 * rel_a + back * (2 * (n - rel_a) - 1)
        tiles.append(wh[rel_b, at])
    partial = jnp.dot(
        hid[...], jnp.concatenate(tiles, axis=0), preferred_element_type=F32
    )
    part_out[...] = partial[tokens:]
    part_copy = remote(part_out, part_in, part_sem.at[0], part_sem.at[1], sibling)
    part_copy.start()

    @pl.when(c != yh)
    def _():
        last_wait(yh, 0)

    last_wait(1 - yh, 0)
    for e in range(1, n):
        last_wait(0, e)
        last_wait(1, e)
    grad = jnp.zeros((ROWS, LANES), F32)
    for y_half in range(2):
        for e in range(n):
            grad = grad + last_in[y_half, e].astype(F32)
    grad_ref[...] = grad * (gain_col * multiplier)

    part_copy.wait_recv()
    for g in range(tokens // 16):
        rows = slice(g * 16, g * 16 + 16)
        both = partial[rows] + part_in[rows, :]
        proj_ref[rows, :] = (both * (inverse[g] * multiplier)).astype(BF16)

    for copy in term_copies + hx_copies + [cx_copy, part_copy]:
        copy.wait_send()
    for d, flip in share_spots[1:]:
        share_copy(d, flip).wait_send()

    @pl.when(c != yh)
    def _():
        share_copy(0, 0).wait_send()
        last_copy(0, 0).wait_send()
        last_copy(0, 1).wait_send()

    @pl.when(c == yh)
    def _():
        last_copy(0, 1 - c).wait_send()

    for d in range(1, n):
        ag1_copy(d).wait_send()
        last_copy(d, 0).wait_send()
        last_copy(d, 1).wait_send()
    for key in ag_slots:
        ag_copy(key).wait_send()
    for key in rs_slots:
        rs_copy(key).wait_send()


def deliver(*refs):
    count = (len(refs) - 1) // 2
    copies = [
        pltpu.make_async_copy(refs[i], refs[count + i], refs[-1].at[i])
        for i in range(count)
    ]
    for copy in copies:
        copy.start()
    for copy in copies:
        copy.wait()


def shards(
    replicas,
    n,
    delta_codes,
    scale_exponents,
    error_feedback,
    base_weights,
    outer_momentum,
    norm_gain,
    hidden_states,
    key_cotangent,
):
    tokens = hidden_states.shape[1]
    width = hidden_states.shape[2]
    half = width // 2
    h = n // 2
    hbm = pl.BlockSpec(memory_space=pltpu.HBM)
    dma = pltpu.SemaphoreType.DMA
    rs_count = 14 if n == 8 else 6
    ag_count = 16 if n == 8 else 8
    outs = pl.pallas_call(
        functools.partial(kernel, replicas, n, tokens),
        out_shape=(
            pltpu.VMEM((tokens, LANES), BF16),
            pltpu.VMEM((ROWS, LANES), F32),
            pltpu.VMEM((ROWS, LANES), F32),
            pltpu.VMEM((ROWS, LANES), F32),
        ),
        in_specs=[hbm] * 8,
        out_specs=(pl.BlockSpec(memory_space=pltpu.VMEM),) * 4,
        scratch_shapes=[
            pltpu.VMEM((ROWS, LANES), jnp.int32),
            pltpu.VMEM((LANES // BLOCK, ROWS), jnp.int32),
            pltpu.VMEM((ROWS, LANES), F32),
            pltpu.VMEM((ROWS, LANES), F32),
            pltpu.VMEM((ROWS, LANES), F32),
            pltpu.VMEM((width // LANES, LANES), F32),
            pltpu.VMEM((tokens, LANES), BF16),
            pltpu.VMEM((2 * tokens, half), BF16),
            pltpu.VMEM((tokens, half), BF16),
            pltpu.VMEM((2 * tokens, LANES), BF16),
            pltpu.VMEM((replicas, ROWS, LANES), F32),
            pltpu.VMEM((ROWS, LANES), BF16),
            pltpu.VMEM((replicas, 2, ROWS, LANES), BF16),
            pltpu.VMEM((n, n, PAIR, LANES), BF16),
            pltpu.VMEM((n, n, PAIR, LANES), F32),
            pltpu.VMEM((rs_count, h, PAIR, LANES), BF16),
            pltpu.VMEM((rs_count, h, PAIR, LANES), BF16),
            pltpu.VMEM((n, 2, ROWS, LANES), BF16),
            pltpu.VMEM((2, n, ROWS, LANES), BF16),
            pltpu.VMEM((tokens, LANES), F32),
            pltpu.VMEM((tokens, LANES), F32),
            dma((9,)),
            dma((replicas,)),
            dma((replicas,)),
            dma((NX,)),
            dma((NX,)),
            dma((2,)),
            dma((replicas, 2)),
            dma((replicas, 2)),
            dma((n,)),
            dma((n,)),
            dma((ag_count,)),
            dma((ag_count,)),
            dma((rs_count,)),
            dma((rs_count,)),
            dma((n, 2)),
            dma((2, n)),
            dma((2,)),
            pltpu.SemaphoreType.REGULAR,
        ],
        compiler_params=pltpu.CompilerParams(
            collective_id=0, has_side_effects=True, vmem_limit_bytes=VMEM_BYTES
        ),
        cost_estimate=pl.CostEstimate(
            flops=4 * tokens * width * LANES,
            bytes_accessed=2 * tokens * width,
            transcendentals=tokens,
        ),
    )(
        delta_codes[0],
        scale_exponents[0].T,
        error_feedback[0],
        base_weights,
        outer_momentum,
        norm_gain.reshape(width // LANES, LANES),
        hidden_states[0],
        key_cotangent[0],
    )
    projected, weight_grad, new_weights, new_momentum = pl.pallas_call(
        deliver,
        out_shape=tuple(jax.ShapeDtypeStruct(o.shape, o.dtype) for o in outs),
        in_specs=[pl.BlockSpec(memory_space=pl.ANY)] * 4,
        out_specs=(hbm,) * 4,
        scratch_shapes=[dma((4,))],
    )(*outs)
    return (projected[None], weight_grad[None], new_weights, new_momentum)


def solution(mesh):
    replicas = mesh.shape["replica"]
    n = math.isqrt(mesh.shape["fsdp"] // 4)
    return jax.shard_map(
        functools.partial(shards, replicas, n),
        mesh=mesh,
        in_specs=(
            P("replica", "fsdp", None),
            P("replica", "fsdp", None),
            P("replica", "fsdp", None),
            P("fsdp", None),
            P("fsdp", None),
            P(),
            P("replica", "fsdp", None),
            P("replica", "fsdp", None),
        ),
        out_specs=(
            P("replica", "fsdp", None),
            P("replica", "fsdp", None),
            P("fsdp", None),
            P("fsdp", None),
        ),
        check_vma=False,
    )
```

```python
import functools
import math

import jax
import jax.numpy as jnp
from jax import lax
from jax.experimental import pallas as pl
from jax.experimental.pallas import tpu as pltpu
from jax.sharding import PartitionSpec as P

BLOCK = 32
ROWS = 32
PAIR = 2 * ROWS
LANES = 128
NX = 4
VMEM_BYTES = 63 * 1024 * 1024
SMALL_BYTES = 4 * 1024 * 1024
MESH = pl.DeviceIdType.MESH
BF16 = jnp.bfloat16
F32 = jnp.float32


def column(line, start):
    shape = (ROWS, line.shape[1])
    lane = lax.broadcasted_iota(jnp.int32, shape, 1)
    row = lax.broadcasted_iota(jnp.int32, shape, 0)
    return jnp.sum(jnp.where(lane == row + start, line, 0.0), axis=1, keepdims=True)


def decode(codes, exponents):
    powers = jnp.where(
        exponents == -6,
        2.0**-6,
        jnp.where(
            exponents == -5, 2.0**-5, jnp.where(exponents == -4, 2.0**-4, 2.0**-3)
        ),
    ).astype(F32)
    lane = lax.broadcasted_iota(jnp.int32, codes.shape, 1)
    scale = jnp.zeros(codes.shape, F32)
    for k in range(codes.shape[1] // BLOCK):
        scale = jnp.where(lane // BLOCK == k, column(powers[k : k + 1], 0), scale)
    magnitude_code = codes % 8
    level = magnitude_code // 2
    fraction = 0.5 * (magnitude_code % 2).astype(F32)
    magnitude = jnp.where(
        level == 0,
        fraction,
        jnp.where(level == 1, 1.0, jnp.where(level == 2, 2.0, 4.0)).astype(F32)
        * (1.0 + fraction),
    )
    return jnp.where(codes >= 8, -magnitude, magnitude) * scale


def ring_plan(n):
    if n == 8:
        return [1], 2, [3]
    if n == 4:
        return [], 1, []
    raise ValueError(n)


def kernel(
    replicas,
    n,
    tokens,
    codes_hbm,
    exps_hbm,
    err_hbm,
    base_hbm,
    mom_hbm,
    gain_hbm,
    hidden_hbm,
    cot_hbm,
    proj_ref,
    grad_ref,
    neww_ref,
    newm_ref,
    codes,
    exps,
    err,
    base,
    mom,
    gain,
    cot,
    hid,
    hother,
    cots,
    terms,
    share,
    shares,
    wh,
    prod,
    rs_out,
    rs_in,
    last_out,
    last_in,
    part_out,
    part_in,
    load_sem,
    term_send,
    term_recv,
    hx_send,
    hx_recv,
    cx_sem,
    share_send,
    share_recv,
    ag1_send,
    ag1_recv,
    ag2_send,
    ag2_recv,
    rs_send,
    rs_recv,
    last_send,
    last_recv,
    part_sem,
    ready_sem,
):
    half = n * n * PAIR
    h = n // 2
    direct, middle, further = ring_plan(n)
    model_width = 2 * half
    multiplier = 1.0 / math.sqrt(model_width)
    r = lax.axis_index("replica")
    index = lax.axis_index("fsdp")
    c = index % 2
    z = (index // 2) % n
    x = (index // (2 * n)) % n
    yh = index // (2 * n * n)
    me_a = (1 - c) * z + c * x
    me_b = (1 - c) * x + c * z

    def device(y_half, a, b, core):
        to_x = (1 - c) * b + c * a
        to_z = (1 - c) * a + c * b
        return (r, ((y_half * n + to_x) * n + to_z) * 2 + core)

    def on_column(step, y_half, core):
        return (lax.rem(r + step, replicas), ((y_half * n + x) * n + z) * 2 + core)

    def along_a(step):
        return device(yh, lax.rem(me_a + step + n, n), me_b, c)

    def along_b(step):
        return device(yh, me_a, lax.rem(me_b + step + n, n), c)

    sibling = on_column(0, yh, 1 - c)

    own = pl.ds(pl.multiple_of(c * half, half), half)
    others = pl.ds(pl.multiple_of((1 - c) * half, half), half)
    small = [
        (codes_hbm, codes),
        (exps_hbm, exps),
        (err_hbm, err),
        (base_hbm, base),
        (mom_hbm, mom),
        (gain_hbm, gain),
        (cot_hbm, cot),
    ]
    loads = [
        pltpu.make_async_copy(src, dst, load_sem.at[i])
        for i, (src, dst) in enumerate(small)
    ]
    load_own = pltpu.make_async_copy(
        hidden_hbm.at[:, own], hid.at[pl.ds(0, tokens)], load_sem.at[len(small)]
    )
    load_other = pltpu.make_async_copy(
        hidden_hbm.at[:, others], hother, load_sem.at[len(small) + 1]
    )

    barrier = pltpu.get_barrier_semaphore()
    partners = [on_column(0, 1 - yh, 0), on_column(0, 1 - yh, 1), sibling]
    for d in range(1, replicas):
        for y_half in range(2):
            for core in range(2):
                partners.append(on_column(d, y_half, core))
    partners += [along_a(d) for d in range(1, n)]
    partners += [along_b(d) for d in range(1, n)]
    for partner in partners:
        pl.semaphore_signal(barrier, inc=1, device_id=partner, device_id_type=MESH)
    for load in loads:
        load.start()
    load_own.start()
    load_other.start()

    for load in loads:
        load.wait()
    term = decode(codes[...], exps[...]) + err[...]
    terms[r] = term
    flat = index * ROWS
    gain_col = column(gain[pl.ds(flat // LANES, 1), :], lax.rem(flat, LANES))
    kept = (base[...] - (0.7 * 0.9 * 0.9) * mom[...]) * (1.0 / replicas)
    my_share = ((kept - (0.7 * 1.9 / replicas) * term) * gain_col).astype(BF16)
    share[...] = my_share

    pl.semaphore_wait(barrier, len(partners))

    def remote(src, dst, send, recv, to):
        return pltpu.make_async_remote_copy(
            src_ref=src,
            dst_ref=dst,
            send_sem=send,
            recv_sem=recv,
            device_id=to,
            device_id_type=MESH,
        )

    def share_copy(d, flip):
        y_half = (1 - yh) * flip + yh * (1 - flip)
        return remote(
            share,
            shares.at[r, c],
            share_send.at[d, flip],
            share_recv.at[r, c],
            on_column(d, y_half, yh),
        )

    share_spots = [(d, flip) for d in range(replicas) for flip in range(2)]
    for d, flip in share_spots[1:]:
        share_copy(d, flip).start()

    @pl.when(c != yh)
    def _():
        share_copy(0, 0).start()

    @pl.when(c == yh)
    def _():
        shares[r, c] = my_share

    hx_copies = []
    piece = tokens // NX
    for i in range(NX):
        copy = remote(
            hidden_hbm.at[pl.ds(i * piece, piece), others],
            hid.at[pl.ds(tokens + i * piece, piece)],
            hx_send.at[i],
            hx_recv.at[i],
            sibling,
        )
        copy.start()
        hx_copies.append(copy)
    term_copies = []
    for d in range(1, replicas):
        copy = remote(
            terms.at[r],
            terms.at[r],
            term_send.at[d],
            term_recv.at[d],
            on_column(d, yh, c),
        )
        copy.start()
        term_copies.append(copy)
    for d in range(1, n):
        pl.semaphore_signal(
            ready_sem, inc=1, device_id=along_b(d), device_id_type=MESH
        )

    load_own.wait()
    load_other.wait()
    inverse = []
    for g in range(tokens // 16):
        rows = pl.ds(g * 16, 16)
        square = jnp.zeros((16, LANES), F32)
        for ref in (hid, hother):
            for j in range(half // LANES):
                wide = ref[rows, j * LANES : (j + 1) * LANES].astype(F32)
                square = square + wide * wide
        mean = jnp.sum(square, axis=1, keepdims=True) * (1.0 / model_width)
        inv = lax.rsqrt(mean + 1e-05)
        inverse.append(inv)
        cots[rows, :] = (cot[rows, :].astype(F32) * inv).astype(BF16)
    cx_copy = remote(
        cots.at[pl.ds(0, tokens)],
        cots.at[pl.ds(tokens, tokens)],
        cx_sem.at[0],
        cx_sem.at[1],
        sibling,
    )
    cx_copy.start()

    for copy in hx_copies:
        copy.wait_recv()
    cx_copy.wait_recv()
    cots_t = cots[...].T
    my_pair = me_a // 2

    def products(offset):
        p = lax.rem(my_pair + offset, h)
        for j in range(0, n, 2):
            tiles = []
            for t in (j, j + 1):
                at = (1 - c) * (t * n * PAIR + p * LANES) + c * (
                    p * 2 * n * PAIR + t * LANES
                )
                tiles.append(hid[:, pl.ds(pl.multiple_of(at, LANES), LANES)])
            out = jnp.dot(
                cots_t,
                jnp.concatenate(tiles, axis=1),
                preferred_element_type=F32,
            ).T
            for i, t in enumerate((j, j + 1)):
                for s in range(2):
                    a = 2 * p + (1 - c) * s + c * (t // h)
                    b = (1 - c) * t + c * (2 * (t % h) + s)
                    start = i * LANES + s * PAIR
                    prod[a, b] = out[start : start + PAIR]

    order = sorted(range(n), key=lambda d: -min(d, n - d))
    groups = [order[:h], order[h:]]
    ways = (1, -1)
    rs_slots = {}
    for q in range(2):
        if middle < h:
            rs_slots["far", q, ways[q], h] = len(rs_slots)
        for s in ways:
            for d in further:
                rs_slots["far", q, s, d] = len(rs_slots)
    for q in range(2):
        for s in ways:
            for d in [middle] + direct:
                rs_slots["near", q, s, d] = len(rs_slots)

    def rs_copy(key):
        kind, _, s, d = key
        slot = rs_slots[key]
        return remote(
            rs_out.at[slot],
            rs_in.at[slot],
            rs_send.at[slot],
            rs_recv.at[slot],
            along_a(s * (d - middle) if kind == "far" else s * d),
        )

    def rs_send_block(key):
        kind, q, s, d = key
        to = lax.rem(me_a + s * d + n, n)
        arrived = []
        if kind == "near" and d == middle:
            arrived = [k for k in rs_slots if k[0] == "far" and k[1:3] == (q, s)]
            for k in arrived:
                rs_copy(k).wait_recv()
        for i, e in enumerate(groups[q]):
            value = prod[to, lax.rem(me_b + e, n)]
            for k in arrived:
                value = value + rs_in[rs_slots[k], i].astype(F32)
            rs_out[rs_slots[key], i] = value.astype(BF16)
        rs_copy(key).start()

    def rs_sends(kind, distances):
        for key in rs_slots:
            if key[0] == kind and key[3] in distances:
                rs_send_block(key)

    def last_copy(e, core):
        return remote(
            last_out.at[e, core],
            last_in.at[yh, e],
            last_send.at[e, core],
            last_recv.at[yh, e],
            device(c, me_a, lax.rem(me_b + e, n), core),
        )

    def rs_last(q):
        keys = [k for k in rs_slots if k[0] == "near" and k[1] == q]
        for k in keys:
            rs_copy(k).wait_recv()
        for i, e in enumerate(groups[q]):
            value = prod[me_a, lax.rem(me_b + e, n)]
            for k in keys:
                value = value + rs_in[rs_slots[k], i].astype(F32)
            value = value.astype(BF16)
            last_out[e, 0] = value[:ROWS]
            last_out[e, 1] = value[ROWS:]
            if e > 0:
                last_copy(e, 0).start()
                last_copy(e, 1).start()
            else:

                @pl.when(c != yh)
                def _():
                    last_copy(0, 0).start()
                    last_copy(0, 1).start()

                @pl.when(c == yh)
                def _():
                    last_copy(0, 1 - c).start()
                    last_in[yh, 0] = last_out[0, c]

    def last_wait(y_half, e):
        spot = last_in.at[y_half, e]
        remote(
            last_out.at[0, 0],
            spot,
            last_send.at[0, 0],
            last_recv.at[y_half, e],
            sibling,
        ).wait_recv()

    nearest = order[::-1]
    place = {d: i for i, d in enumerate(nearest)}

    def ag1_copy(d):
        return remote(
            wh.at[0, 0],
            wh.at[0, place[n - d]],
            ag1_send.at[d],
            ag1_recv.at[d],
            along_a(d),
        )

    ag_slots = {}
    for g in range(2):
        for s in ways:
            for d in [middle] + direct:
                ag_slots["near", g, s, d] = len(ag_slots)
        for s in ways:
            for d in further + [h]:
                ag_slots["far", g, s, d] = len(ag_slots)

    def ag_copy(key):
        kind, g, s, d = key
        first, count = g * h, h
        if d == h:
            count = h // 2
            first += count * (s < 0)
        blocks = pl.ds(first, count)
        came, hops = (0, d) if kind == "near" else (middle, d - middle)
        slot = ag_slots[key]
        return remote(
            wh.at[(-s * came) % n, blocks],
            wh.at[(-s * d) % n, blocks],
            ag2_send.at[slot],
            ag2_recv.at[slot],
            along_b(s * hops),
        )

    def ag_near(g):
        for d in nearest[g * h : (g + 1) * h]:
            if d > 0:
                ag1_copy(n - d).wait_recv()
        for key in ag_slots:
            if key[:2] == ("near", g):
                ag_copy(key).start()

    def ag_far(g):
        for s in ways:
            ag_copy(("near", g, s, middle)).wait_recv()
            for d in further + [h]:
                ag_copy(("far", g, s, d)).start()

    pairs = sorted(range(h), key=lambda d: -min(d, h - d))
    for offset in pairs[:-1]:
        products(offset)
    rs_sends("far", [h])
    rs_sends("far", further)
    products(pairs[-1])

    @pl.when(c != yh)
    def _():
        remote(
            share, shares.at[r, c], share_send.at[0, 0], share_recv.at[r, c], sibling
        ).wait_recv()

    for d in range(replicas):
        for other in range(2):
            if (d, other) != (0, 0):
                source = lax.rem(r + d, replicas)
                core = (c + other) % 2
                remote(
                    share,
                    shares.at[source, core],
                    share_send.at[0, 0],
                    share_recv.at[source, core],
                    sibling,
                ).wait_recv()
    for core in range(2):
        rows64 = shares[0, core].astype(F32)
        for d in range(1, replicas):
            rows64 = rows64 + shares[d, core].astype(F32)
        wh[0, 0, pl.ds(core * ROWS, ROWS)] = rows64.astype(BF16)
    for d in nearest[1:]:
        ag1_copy(d).start()

    rs_sends("near", direct)
    ag_near(0)
    rs_sends("near", [middle])
    ag_near(1)
    ag_far(0)

    for copy in term_copies:
        copy.wait_recv()
    summed = terms[0]
    for d in range(1, replicas):
        summed = summed + terms[d]
    outer_grad = summed / replicas
    new_momentum = 0.9 * mom[...] + outer_grad
    newm_ref[...] = new_momentum
    neww_ref[...] = base[...] - 0.7 * (outer_grad + 0.9 * new_momentum)

    pl.semaphore_wait(ready_sem, n - 1)
    rs_last(0)
    rs_last(1)
    ag_far(1)
    for key in ag_slots:
        if key[0] == "far" or key[3] != middle:
            ag_copy(key).wait_recv()

    pieces = []
    for tx in range(n):
        for tz in range(n):
            a = (1 - c) * tz + c * tx
            b = (1 - c) * tx + c * tz
            rel_a = lax.rem(a - me_a + n, n)
            rel_b = lax.rem(b - me_b + n, n)
            pieces.append((rel_b, rel_a))
    tiles = []
    for rel_b, rel_a in pieces:
        back = rel_a // h
        at = (1 - back) * 2 * rel_a + back * (2 * (n - rel_a) - 1)
        tiles.append(wh[rel_b, at])
    partial = jnp.dot(
        hid[...], jnp.concatenate(tiles, axis=0), preferred_element_type=F32
    )
    part_out[...] = partial[tokens:]
    part_copy = remote(part_out, part_in, part_sem.at[0], part_sem.at[1], sibling)
    part_copy.start()

    @pl.when(c != yh)
    def _():
        last_wait(yh, 0)

    last_wait(1 - yh, 0)
    for e in range(1, n):
        last_wait(0, e)
        last_wait(1, e)
    grad = jnp.zeros((ROWS, LANES), F32)
    for y_half in range(2):
        for e in range(n):
            grad = grad + last_in[y_half, e].astype(F32)
    grad_ref[...] = grad * (gain_col * multiplier)

    part_copy.wait_recv()
    for g in range(tokens // 16):
        rows = slice(g * 16, g * 16 + 16)
        both = partial[rows] + part_in[rows, :]
        proj_ref[rows, :] = (both * (inverse[g] * multiplier)).astype(BF16)

    for copy in term_copies + hx_copies + [cx_copy, part_copy]:
        copy.wait_send()
    for d, flip in share_spots[1:]:
        share_copy(d, flip).wait_send()

    @pl.when(c != yh)
    def _():
        share_copy(0, 0).wait_send()
        last_copy(0, 0).wait_send()
        last_copy(0, 1).wait_send()

    @pl.when(c == yh)
    def _():
        last_copy(0, 1 - c).wait_send()

    for d in range(1, n):
        ag1_copy(d).wait_send()
        last_copy(d, 0).wait_send()
        last_copy(d, 1).wait_send()
    for key in ag_slots:
        ag_copy(key).wait_send()
    for key in rs_slots:
        rs_copy(key).wait_send()


def deliver(*refs):
    count = (len(refs) - 1) // 2
    copies = [
        pltpu.make_async_copy(refs[i], refs[count + i], refs[-1].at[i])
        for i in range(count)
    ]
    for copy in copies:
        copy.start()
    for copy in copies:
        copy.wait()


def shards(
    replicas,
    n,
    delta_codes,
    scale_exponents,
    error_feedback,
    base_weights,
    outer_momentum,
    norm_gain,
    hidden_states,
    key_cotangent,
):
    tokens = hidden_states.shape[1]
    width = hidden_states.shape[2]
    half = width // 2
    h = n // 2
    hbm = pl.BlockSpec(memory_space=pltpu.HBM)
    dma = pltpu.SemaphoreType.DMA
    rs_count = 14 if n == 8 else 6
    ag_count = 16 if n == 8 else 8
    outs = pl.pallas_call(
        functools.partial(kernel, replicas, n, tokens),
        out_shape=(
            pltpu.VMEM((tokens, LANES), BF16),
            pltpu.VMEM((ROWS, LANES), F32),
            pltpu.VMEM((ROWS, LANES), F32),
            pltpu.VMEM((ROWS, LANES), F32),
        ),
        in_specs=[hbm] * 8,
        out_specs=(pl.BlockSpec(memory_space=pltpu.VMEM),) * 4,
        scratch_shapes=[
            pltpu.VMEM((ROWS, LANES), jnp.int32),
            pltpu.VMEM((LANES // BLOCK, ROWS), jnp.int32),
            pltpu.VMEM((ROWS, LANES), F32),
            pltpu.VMEM((ROWS, LANES), F32),
            pltpu.VMEM((ROWS, LANES), F32),
            pltpu.VMEM((width // LANES, LANES), F32),
            pltpu.VMEM((tokens, LANES), BF16),
            pltpu.VMEM((2 * tokens, half), BF16),
            pltpu.VMEM((tokens, half), BF16),
            pltpu.VMEM((2 * tokens, LANES), BF16),
            pltpu.VMEM((replicas, ROWS, LANES), F32),
            pltpu.VMEM((ROWS, LANES), BF16),
            pltpu.VMEM((replicas, 2, ROWS, LANES), BF16),
            pltpu.VMEM((n, n, PAIR, LANES), BF16),
            pltpu.VMEM((n, n, PAIR, LANES), F32),
            pltpu.VMEM((rs_count, h, PAIR, LANES), BF16),
            pltpu.VMEM((rs_count, h, PAIR, LANES), BF16),
            pltpu.VMEM((n, 2, ROWS, LANES), BF16),
            pltpu.VMEM((2, n, ROWS, LANES), BF16),
            pltpu.VMEM((tokens, LANES), F32),
            pltpu.VMEM((tokens, LANES), F32),
            dma((9,)),
            dma((replicas,)),
            dma((replicas,)),
            dma((NX,)),
            dma((NX,)),
            dma((2,)),
            dma((replicas, 2)),
            dma((replicas, 2)),
            dma((n,)),
            dma((n,)),
            dma((ag_count,)),
            dma((ag_count,)),
            dma((rs_count,)),
            dma((rs_count,)),
            dma((n, 2)),
            dma((2, n)),
            dma((2,)),
            pltpu.SemaphoreType.REGULAR,
        ],
        compiler_params=pltpu.CompilerParams(
            collective_id=0, has_side_effects=True, vmem_limit_bytes=VMEM_BYTES
        ),
        cost_estimate=pl.CostEstimate(
            flops=4 * tokens * width * LANES,
            bytes_accessed=2 * tokens * width,
            transcendentals=tokens,
        ),
    )(
        delta_codes[0],
        scale_exponents[0].T,
        error_feedback[0],
        base_weights,
        outer_momentum,
        norm_gain.reshape(width // LANES, LANES),
        hidden_states[0],
        key_cotangent[0],
    )
    projected, weight_grad, new_weights, new_momentum = pl.pallas_call(
        deliver,
        out_shape=tuple(jax.ShapeDtypeStruct(o.shape, o.dtype) for o in outs),
        in_specs=[pl.BlockSpec(memory_space=pl.ANY)] * 4,
        out_specs=(hbm,) * 4,
        scratch_shapes=[dma((4,))],
        compiler_params=pltpu.CompilerParams(vmem_limit_bytes=SMALL_BYTES),
    )(*outs)
    return (projected[None], weight_grad[None], new_weights, new_momentum)


def solution(mesh):
    replicas = mesh.shape["replica"]
    n = math.isqrt(mesh.shape["fsdp"] // 4)
    return jax.shard_map(
        functools.partial(shards, replicas, n),
        mesh=mesh,
        in_specs=(
            P("replica", "fsdp", None),
            P("replica", "fsdp", None),
            P("replica", "fsdp", None),
            P("fsdp", None),
            P("fsdp", None),
            P(),
            P("replica", "fsdp", None),
            P("replica", "fsdp", None),
        ),
        out_specs=(
            P("replica", "fsdp", None),
            P("replica", "fsdp", None),
            P("fsdp", None),
            P("fsdp", None),
        ),
        check_vma=False,
    )
```

```python
import functools
import math

import jax
import jax.numpy as jnp
from jax import lax
from jax.experimental import pallas as pl
from jax.experimental.pallas import tpu as pltpu
from jax.sharding import PartitionSpec as P

BLOCK = 32
ROWS = 32
PAIR = 2 * ROWS
LANES = 128
NX = 4
VMEM_BYTES = 63 * 1024 * 1024
SMALL_BYTES = 4 * 1024 * 1024
MESH = pl.DeviceIdType.MESH
BF16 = jnp.bfloat16
F32 = jnp.float32


def column(line, start):
    shape = (ROWS, line.shape[1])
    lane = lax.broadcasted_iota(jnp.int32, shape, 1)
    row = lax.broadcasted_iota(jnp.int32, shape, 0)
    return jnp.sum(jnp.where(lane == row + start, line, 0.0), axis=1, keepdims=True)


def decode(codes, exponents):
    powers = jnp.where(
        exponents == -6,
        2.0**-6,
        jnp.where(
            exponents == -5, 2.0**-5, jnp.where(exponents == -4, 2.0**-4, 2.0**-3)
        ),
    ).astype(F32)
    lane = lax.broadcasted_iota(jnp.int32, codes.shape, 1)
    scale = jnp.zeros(codes.shape, F32)
    for k in range(codes.shape[1] // BLOCK):
        scale = jnp.where(lane // BLOCK == k, column(powers[k : k + 1], 0), scale)
    magnitude_code = codes % 8
    level = magnitude_code // 2
    fraction = 0.5 * (magnitude_code % 2).astype(F32)
    magnitude = jnp.where(
        level == 0,
        fraction,
        jnp.where(level == 1, 1.0, jnp.where(level == 2, 2.0, 4.0)).astype(F32)
        * (1.0 + fraction),
    )
    return jnp.where(codes >= 8, -magnitude, magnitude) * scale


def ring_plan(n):
    if n == 8:
        return [1], 2, [3]
    if n == 4:
        return [], 1, []
    raise ValueError(n)


def kernel(
    replicas,
    n,
    tokens,
    codes_hbm,
    exps_hbm,
    err_hbm,
    base_hbm,
    mom_hbm,
    gain_hbm,
    hidden_hbm,
    cot_hbm,
    proj_ref,
    grad_ref,
    neww_ref,
    newm_ref,
    codes,
    exps,
    err,
    base,
    mom,
    gain,
    cot,
    hid,
    hother,
    cots,
    terms,
    share,
    shares,
    wh,
    prod,
    rs_out,
    rs_in,
    last_out,
    last_in,
    part_out,
    part_in,
    load_sem,
    term_send,
    term_recv,
    hx_send,
    hx_recv,
    cx_sem,
    share_send,
    share_recv,
    ag1_send,
    ag1_recv,
    ag2_send,
    ag2_recv,
    rs_send,
    rs_recv,
    last_send,
    last_recv,
    part_sem,
    ready_sem,
):
    half = n * n * PAIR
    h = n // 2
    direct, middle, further = ring_plan(n)
    model_width = 2 * half
    multiplier = 1.0 / math.sqrt(model_width)
    r = lax.axis_index("replica")
    index = lax.axis_index("fsdp")
    c = index % 2
    z = (index // 2) % n
    x = (index // (2 * n)) % n
    yh = index // (2 * n * n)
    me_a = (1 - c) * z + c * x
    me_b = (1 - c) * x + c * z

    def device(y_half, a, b, core):
        to_x = (1 - c) * b + c * a
        to_z = (1 - c) * a + c * b
        return (r, ((y_half * n + to_x) * n + to_z) * 2 + core)

    def on_column(step, y_half, core):
        return (lax.rem(r + step, replicas), ((y_half * n + x) * n + z) * 2 + core)

    def along_a(step):
        return device(yh, lax.rem(me_a + step + n, n), me_b, c)

    def along_b(step):
        return device(yh, me_a, lax.rem(me_b + step + n, n), c)

    sibling = on_column(0, yh, 1 - c)

    own = pl.ds(pl.multiple_of(c * half, half), half)
    others = pl.ds(pl.multiple_of((1 - c) * half, half), half)
    small = [
        (codes_hbm, codes),
        (exps_hbm, exps),
        (err_hbm, err),
        (base_hbm, base),
        (mom_hbm, mom),
        (gain_hbm, gain),
        (cot_hbm, cot),
    ]
    loads = [
        pltpu.make_async_copy(src, dst, load_sem.at[i])
        for i, (src, dst) in enumerate(small)
    ]
    load_own = pltpu.make_async_copy(
        hidden_hbm.at[:, own], hid.at[pl.ds(0, tokens)], load_sem.at[len(small)]
    )
    load_other = pltpu.make_async_copy(
        hidden_hbm.at[:, others], hother, load_sem.at[len(small) + 1]
    )

    barrier = pltpu.get_barrier_semaphore()
    partners = [on_column(0, 1 - yh, 0), on_column(0, 1 - yh, 1), sibling]
    for d in range(1, replicas):
        for y_half in range(2):
            for core in range(2):
                partners.append(on_column(d, y_half, core))
    partners += [along_a(d) for d in range(1, n)]
    partners += [along_b(d) for d in range(1, n)]
    for partner in partners:
        pl.semaphore_signal(barrier, inc=1, device_id=partner, device_id_type=MESH)
    for load in loads:
        load.start()
    load_own.start()
    load_other.start()

    for load in loads:
        load.wait()
    term = decode(codes[...], exps[...]) + err[...]
    terms[r] = term
    flat = index * ROWS
    gain_col = column(gain[pl.ds(flat // LANES, 1), :], lax.rem(flat, LANES))
    kept = (base[...] - (0.7 * 0.9 * 0.9) * mom[...]) * (1.0 / replicas)
    my_share = ((kept - (0.7 * 1.9 / replicas) * term) * gain_col).astype(BF16)
    share[...] = my_share

    pl.semaphore_wait(barrier, len(partners))

    def remote(src, dst, send, recv, to):
        return pltpu.make_async_remote_copy(
            src_ref=src,
            dst_ref=dst,
            send_sem=send,
            recv_sem=recv,
            device_id=to,
            device_id_type=MESH,
        )

    def share_copy(d, flip):
        y_half = (1 - yh) * flip + yh * (1 - flip)
        return remote(
            share,
            shares.at[r, c],
            share_send.at[d, flip],
            share_recv.at[r, c],
            on_column(d, y_half, yh),
        )

    share_spots = [(d, flip) for d in range(replicas) for flip in range(2)]
    for d, flip in share_spots[1:]:
        share_copy(d, flip).start()

    @pl.when(c != yh)
    def _():
        share_copy(0, 0).start()

    @pl.when(c == yh)
    def _():
        shares[r, c] = my_share

    hx_copies = []
    piece = tokens // NX
    for i in range(NX):
        copy = remote(
            hidden_hbm.at[pl.ds(i * piece, piece), others],
            hid.at[pl.ds(tokens + i * piece, piece)],
            hx_send.at[i],
            hx_recv.at[i],
            sibling,
        )
        copy.start()
        hx_copies.append(copy)
    term_copies = []
    for d in range(1, replicas):
        copy = remote(
            terms.at[r],
            terms.at[r],
            term_send.at[d],
            term_recv.at[d],
            on_column(d, yh, c),
        )
        copy.start()
        term_copies.append(copy)
    for d in range(1, n):
        pl.semaphore_signal(
            ready_sem, inc=1, device_id=along_b(d), device_id_type=MESH
        )

    load_own.wait()
    load_other.wait()
    inverse = []
    for g in range(tokens // 16):
        rows = pl.ds(g * 16, 16)
        square = jnp.zeros((16, LANES), F32)
        for ref in (hid, hother):
            for j in range(half // LANES):
                wide = ref[rows, j * LANES : (j + 1) * LANES].astype(F32)
                square = square + wide * wide
        mean = jnp.sum(square, axis=1, keepdims=True) * (1.0 / model_width)
        inv = lax.rsqrt(mean + 1e-05)
        inverse.append(inv)
        cots[rows, :] = (cot[rows, :].astype(F32) * inv).astype(BF16)
    cx_copy = remote(
        cots.at[pl.ds(0, tokens)],
        cots.at[pl.ds(tokens, tokens)],
        cx_sem.at[0],
        cx_sem.at[1],
        sibling,
    )
    cx_copy.start()

    for copy in hx_copies:
        copy.wait_recv()
    cx_copy.wait_recv()
    cots_t = cots[...].T
    my_pair = me_a // 2

    def products(offset):
        p = lax.rem(my_pair + offset, h)
        for j in range(0, n, 2):
            tiles = []
            for t in (j, j + 1):
                at = (1 - c) * (t * n * PAIR + p * LANES) + c * (
                    p * 2 * n * PAIR + t * LANES
                )
                tiles.append(hid[:, pl.ds(pl.multiple_of(at, LANES), LANES)])
            out = jnp.dot(
                cots_t,
                jnp.concatenate(tiles, axis=1),
                preferred_element_type=F32,
            ).T
            for i, t in enumerate((j, j + 1)):
                for s in range(2):
                    a = 2 * p + (1 - c) * s + c * (t // h)
                    b = (1 - c) * t + c * (2 * (t % h) + s)
                    start = i * LANES + s * PAIR
                    prod[a, b] = out[start : start + PAIR]

    order = sorted(range(n), key=lambda d: -min(d, n - d))
    groups = [order[:h], order[h:]]
    ways = (1, -1)
    rs_slots = {}
    for q in range(2):
        if middle < h:
            rs_slots["far", q, ways[q], h] = len(rs_slots)
        for s in ways:
            for d in further:
                rs_slots["far", q, s, d] = len(rs_slots)
    for q in range(2):
        for s in ways:
            for d in [middle] + direct:
                rs_slots["near", q, s, d] = len(rs_slots)

    def rs_copy(key):
        kind, _, s, d = key
        slot = rs_slots[key]
        return remote(
            rs_out.at[slot],
            rs_in.at[slot],
            rs_send.at[slot],
            rs_recv.at[slot],
            along_a(s * (d - middle) if kind == "far" else s * d),
        )

    def rs_send_block(key):
        kind, q, s, d = key
        to = lax.rem(me_a + s * d + n, n)
        arrived = []
        if kind == "near" and d == middle:
            arrived = [k for k in rs_slots if k[0] == "far" and k[1:3] == (q, s)]
            for k in arrived:
                rs_copy(k).wait_recv()
        for i, e in enumerate(groups[q]):
            value = prod[to, lax.rem(me_b + e, n)]
            for k in arrived:
                value = value + rs_in[rs_slots[k], i].astype(F32)
            rs_out[rs_slots[key], i] = value.astype(BF16)
        rs_copy(key).start()

    def rs_sends(kind, distances):
        for key in rs_slots:
            if key[0] == kind and key[3] in distances:
                rs_send_block(key)

    def last_copy(e, core):
        return remote(
            last_out.at[e, core],
            last_in.at[yh, e],
            last_send.at[e, core],
            last_recv.at[yh, e],
            device(c, me_a, lax.rem(me_b + e, n), core),
        )

    def rs_last(q):
        keys = [k for k in rs_slots if k[0] == "near" and k[1] == q]
        for k in keys:
            rs_copy(k).wait_recv()
        for i, e in enumerate(groups[q]):
            value = prod[me_a, lax.rem(me_b + e, n)]
            for k in keys:
                value = value + rs_in[rs_slots[k], i].astype(F32)
            value = value.astype(BF16)
            last_out[e, 0] = value[:ROWS]
            last_out[e, 1] = value[ROWS:]
            if e > 0:
                last_copy(e, 0).start()
                last_copy(e, 1).start()
            else:

                @pl.when(c != yh)
                def _():
                    last_copy(0, 0).start()
                    last_copy(0, 1).start()

                @pl.when(c == yh)
                def _():
                    last_copy(0, 1 - c).start()
                    last_in[yh, 0] = last_out[0, c]

    def last_wait(y_half, e):
        spot = last_in.at[y_half, e]
        remote(
            last_out.at[0, 0],
            spot,
            last_send.at[0, 0],
            last_recv.at[y_half, e],
            sibling,
        ).wait_recv()

    nearest = order[::-1]
    place = {d: i for i, d in enumerate(nearest)}

    def ag1_copy(d):
        return remote(
            wh.at[0, 0],
            wh.at[0, place[n - d]],
            ag1_send.at[d],
            ag1_recv.at[d],
            along_a(d),
        )

    ag_slots = {}
    for g in range(2):
        for s in ways:
            for d in [middle] + direct:
                ag_slots["near", g, s, d] = len(ag_slots)
        for s in ways:
            for d in further + [h]:
                ag_slots["far", g, s, d] = len(ag_slots)

    def ag_copy(key):
        kind, g, s, d = key
        first, count = g * h, h
        if d == h:
            count = h // 2
            first += count * (s < 0)
        blocks = pl.ds(first, count)
        came, hops = (0, d) if kind == "near" else (middle, d - middle)
        slot = ag_slots[key]
        return remote(
            wh.at[(-s * came) % n, blocks],
            wh.at[(-s * d) % n, blocks],
            ag2_send.at[slot],
            ag2_recv.at[slot],
            along_b(s * hops),
        )

    def ag_near(g):
        for d in nearest[g * h : (g + 1) * h]:
            if d > 0:
                ag1_copy(n - d).wait_recv()
        for key in ag_slots:
            if key[:2] == ("near", g):
                ag_copy(key).start()

    def ag_far(g):
        for s in ways:
            ag_copy(("near", g, s, middle)).wait_recv()
            for d in further + [h]:
                ag_copy(("far", g, s, d)).start()

    pairs = sorted(range(h), key=lambda d: -min(d, h - d))
    for offset in pairs[:-1]:
        products(offset)
    rs_sends("far", [h])
    rs_sends("far", further)
    products(pairs[-1])

    @pl.when(c != yh)
    def _():
        remote(
            share, shares.at[r, c], share_send.at[0, 0], share_recv.at[r, c], sibling
        ).wait_recv()

    for d in range(replicas):
        for other in range(2):
            if (d, other) != (0, 0):
                source = lax.rem(r + d, replicas)
                core = (c + other) % 2
                remote(
                    share,
                    shares.at[source, core],
                    share_send.at[0, 0],
                    share_recv.at[source, core],
                    sibling,
                ).wait_recv()
    for core in range(2):
        rows64 = shares[0, core].astype(F32)
        for d in range(1, replicas):
            rows64 = rows64 + shares[d, core].astype(F32)
        wh[0, 0, pl.ds(core * ROWS, ROWS)] = rows64.astype(BF16)
    for d in nearest[1:]:
        ag1_copy(d).start()

    ag_near(0)
    rs_sends("near", [middle])
    ag_near(1)
    rs_sends("near", direct)
    ag_far(0)

    for copy in term_copies:
        copy.wait_recv()
    summed = terms[0]
    for d in range(1, replicas):
        summed = summed + terms[d]
    outer_grad = summed / replicas
    new_momentum = 0.9 * mom[...] + outer_grad
    newm_ref[...] = new_momentum
    neww_ref[...] = base[...] - 0.7 * (outer_grad + 0.9 * new_momentum)

    pl.semaphore_wait(ready_sem, n - 1)
    rs_last(0)
    rs_last(1)
    ag_far(1)
    for key in ag_slots:
        if key[0] == "far" or key[3] != middle:
            ag_copy(key).wait_recv()

    pieces = []
    for tx in range(n):
        for tz in range(n):
            a = (1 - c) * tz + c * tx
            b = (1 - c) * tx + c * tz
            rel_a = lax.rem(a - me_a + n, n)
            rel_b = lax.rem(b - me_b + n, n)
            pieces.append((rel_b, rel_a))
    tiles = []
    for rel_b, rel_a in pieces:
        back = rel_a // h
        at = (1 - back) * 2 * rel_a + back * (2 * (n - rel_a) - 1)
        tiles.append(wh[rel_b, at])
    partial = jnp.dot(
        hid[...], jnp.concatenate(tiles, axis=0), preferred_element_type=F32
    )
    part_out[...] = partial[tokens:]
    part_copy = remote(part_out, part_in, part_sem.at[0], part_sem.at[1], sibling)
    part_copy.start()

    @pl.when(c != yh)
    def _():
        last_wait(yh, 0)

    last_wait(1 - yh, 0)
    for e in range(1, n):
        last_wait(0, e)
        last_wait(1, e)
    grad = jnp.zeros((ROWS, LANES), F32)
    for y_half in range(2):
        for e in range(n):
            grad = grad + last_in[y_half, e].astype(F32)
    grad_ref[...] = grad * (gain_col * multiplier)

    part_copy.wait_recv()
    for g in range(tokens // 16):
        rows = slice(g * 16, g * 16 + 16)
        both = partial[rows] + part_in[rows, :]
        proj_ref[rows, :] = (both * (inverse[g] * multiplier)).astype(BF16)

    for copy in term_copies + hx_copies + [cx_copy, part_copy]:
        copy.wait_send()
    for d, flip in share_spots[1:]:
        share_copy(d, flip).wait_send()

    @pl.when(c != yh)
    def _():
        share_copy(0, 0).wait_send()
        last_copy(0, 0).wait_send()
        last_copy(0, 1).wait_send()

    @pl.when(c == yh)
    def _():
        last_copy(0, 1 - c).wait_send()

    for d in range(1, n):
        ag1_copy(d).wait_send()
        last_copy(d, 0).wait_send()
        last_copy(d, 1).wait_send()
    for key in ag_slots:
        ag_copy(key).wait_send()
    for key in rs_slots:
        rs_copy(key).wait_send()


def deliver(*refs):
    count = (len(refs) - 1) // 2
    copies = [
        pltpu.make_async_copy(refs[i], refs[count + i], refs[-1].at[i])
        for i in range(count)
    ]
    for copy in copies:
        copy.start()
    for copy in copies:
        copy.wait()


def shards(
    replicas,
    n,
    delta_codes,
    scale_exponents,
    error_feedback,
    base_weights,
    outer_momentum,
    norm_gain,
    hidden_states,
    key_cotangent,
):
    tokens = hidden_states.shape[1]
    width = hidden_states.shape[2]
    half = width // 2
    h = n // 2
    hbm = pl.BlockSpec(memory_space=pltpu.HBM)
    dma = pltpu.SemaphoreType.DMA
    rs_count = 14 if n == 8 else 6
    ag_count = 16 if n == 8 else 8
    outs = pl.pallas_call(
        functools.partial(kernel, replicas, n, tokens),
        out_shape=(
            pltpu.VMEM((tokens, LANES), BF16),
            pltpu.VMEM((ROWS, LANES), F32),
            pltpu.VMEM((ROWS, LANES), F32),
            pltpu.VMEM((ROWS, LANES), F32),
        ),
        in_specs=[hbm] * 8,
        out_specs=(pl.BlockSpec(memory_space=pltpu.VMEM),) * 4,
        scratch_shapes=[
            pltpu.VMEM((ROWS, LANES), jnp.int32),
            pltpu.VMEM((LANES // BLOCK, ROWS), jnp.int32),
            pltpu.VMEM((ROWS, LANES), F32),
            pltpu.VMEM((ROWS, LANES), F32),
            pltpu.VMEM((ROWS, LANES), F32),
            pltpu.VMEM((width // LANES, LANES), F32),
            pltpu.VMEM((tokens, LANES), BF16),
            pltpu.VMEM((2 * tokens, half), BF16),
            pltpu.VMEM((tokens, half), BF16),
            pltpu.VMEM((2 * tokens, LANES), BF16),
            pltpu.VMEM((replicas, ROWS, LANES), F32),
            pltpu.VMEM((ROWS, LANES), BF16),
            pltpu.VMEM((replicas, 2, ROWS, LANES), BF16),
            pltpu.VMEM((n, n, PAIR, LANES), BF16),
            pltpu.VMEM((n, n, PAIR, LANES), F32),
            pltpu.VMEM((rs_count, h, PAIR, LANES), BF16),
            pltpu.VMEM((rs_count, h, PAIR, LANES), BF16),
            pltpu.VMEM((n, 2, ROWS, LANES), BF16),
            pltpu.VMEM((2, n, ROWS, LANES), BF16),
            pltpu.VMEM((tokens, LANES), F32),
            pltpu.VMEM((tokens, LANES), F32),
            dma((9,)),
            dma((replicas,)),
            dma((replicas,)),
            dma((NX,)),
            dma((NX,)),
            dma((2,)),
            dma((replicas, 2)),
            dma((replicas, 2)),
            dma((n,)),
            dma((n,)),
            dma((ag_count,)),
            dma((ag_count,)),
            dma((rs_count,)),
            dma((rs_count,)),
            dma((n, 2)),
            dma((2, n)),
            dma((2,)),
            pltpu.SemaphoreType.REGULAR,
        ],
        compiler_params=pltpu.CompilerParams(
            collective_id=0, has_side_effects=True, vmem_limit_bytes=VMEM_BYTES
        ),
        cost_estimate=pl.CostEstimate(
            flops=4 * tokens * width * LANES,
            bytes_accessed=2 * tokens * width,
            transcendentals=tokens,
        ),
    )(
        delta_codes[0],
        scale_exponents[0].T,
        error_feedback[0],
        base_weights,
        outer_momentum,
        norm_gain.reshape(width // LANES, LANES),
        hidden_states[0],
        key_cotangent[0],
    )
    projected, weight_grad, new_weights, new_momentum = pl.pallas_call(
        deliver,
        out_shape=tuple(jax.ShapeDtypeStruct(o.shape, o.dtype) for o in outs),
        in_specs=[pl.BlockSpec(memory_space=pl.ANY)] * 4,
        out_specs=(hbm,) * 4,
        scratch_shapes=[dma((4,))],
        compiler_params=pltpu.CompilerParams(vmem_limit_bytes=SMALL_BYTES),
    )(*outs)
    return (projected[None], weight_grad[None], new_weights, new_momentum)


def solution(mesh):
    replicas = mesh.shape["replica"]
    n = math.isqrt(mesh.shape["fsdp"] // 4)
    return jax.shard_map(
        functools.partial(shards, replicas, n),
        mesh=mesh,
        in_specs=(
            P("replica", "fsdp", None),
            P("replica", "fsdp", None),
            P("replica", "fsdp", None),
            P("fsdp", None),
            P("fsdp", None),
            P(),
            P("replica", "fsdp", None),
            P("replica", "fsdp", None),
        ),
        out_specs=(
            P("replica", "fsdp", None),
            P("replica", "fsdp", None),
            P("fsdp", None),
            P("fsdp", None),
        ),
        check_vma=False,
    )
```
